1024 devices in a mesh: dp: 16 (over z, x_hi), ctx: 8 (over y), tp: 8 (over x_lo, core).
Axes of the slice: x: 8 (x_hi: 2, x_lo: 4; x = x_hi * 4 + x_lo), y: 8, z: 8, core: 2. Of those that a mesh axis runs over, the one named last changes fastest.
Arguments:
- tokens: bfloat16 [8192, 3072], P(('dp', 'ctx'), 'tp'), may hold values from -6 to 6
- expert_ids: int32 [8192, 2], P(('dp', 'ctx')), may hold values from 0 to 7, all different within a row; in each aligned block of 64 rows (0 to 63, 64 to 127, ...) at most 18 rows name the same one
- weights: bfloat16 [8, 3072, 8192], P('ctx', None, 'tp'), may hold values from -0.109375 to 0.109375
- cotangent: bfloat16 [16, 8, 144, 8192], P('dp', 'ctx', None, 'tp'), may hold values from -6 to 6
Outputs:
- hidden: bfloat16 [16, 8, 144, 8192], P('dp', 'ctx', None, 'tp')
- weight_grad: bfloat16 [8, 3072, 8192], P('ctx', 'dp', 'tp')
- token_grad: bfloat16 [8192, 3072], P(('dp', 'ctx'), 'tp')
The draws below stay inside these ranges and needn't reach their ends.
Inputs may be any that keep to these rules, and one draw needn't show every extreme that they name: `expert_ids`: the two experts of a token differ. Among the tokens of one aligned block of 64 tokens no expert is named more than 18 times, and in some block one expert is named exactly 18 times.
All inputs are finite; a program needn't handle non-finite values.
Results may differ from the reference program's by a relative error of at most 0.02.
Values may be sent and summed in bfloat16 or wider, within the bound.
A program may use at most 64 MiB of HBM per device.

```python
import math
import jax
import jax.numpy as jnp
import numpy as np
from jax import lax

D = 3072
FF = 8192
TOK_DEV = 64
EXPERTS = 8
CAP = 18
SLOTS = 144
GROUPS = 16
TOKENS = 8192
N_DP = 16
N_CTX = 8
N_TP = 8


def levels(key, shape, cuts, smallest, high):
    level, own = 1.0, jax.random.fold_in(key, 6)
    for axis_at, blocks in cuts:
        draws = jnp.exp(jax.random.uniform(jax.random.fold_in(own, axis_at), (blocks,), jnp.float32, smallest / len(cuts), high / len(cuts)))
        level = level * jnp.repeat(draws, shape[axis_at] // blocks).reshape([-1 if axis == axis_at else 1 for axis in range(len(shape))])
    return level


def assign_block(stream_key, own, number, rows, amount, top, limit, skew):
    sequence = jax.random.permutation(stream_key, amount)
    packed, common = portions_of(amount, rows * top, limit, skew, True), portions_of(amount, rows * top, limit, skew, False)
    places = jnp.arange(amount)

    def named(tallies, rotation):
        used = int((tallies > 0).sum())
        fixed = max(1, used // 4)
        moved = fixed + (places - fixed + rotation * (used - fixed)) % max(1, amount - fixed)
        return jnp.zeros((amount,), jnp.int32).at[sequence[jnp.where(places < fixed, places, moved)]].set(jnp.asarray(tallies, jnp.int32))

    tallies = jnp.where(number % 4 == 0, named(packed, number // 4), named(common, number - number // 4 - 1))
    mixed = jax.random.permutation(jax.random.fold_in(own, 3), amount)
    donor, receiver = mixed[0:amount // 2 * 2:2], mixed[1:amount // 2 * 2:2]
    slack = jnp.minimum(tallies[donor] - 1, limit - tallies[receiver]) // 2
    slack = jnp.where((donor == sequence[0]) | (receiver == sequence[0]) | (tallies[receiver] == 0), 0, jnp.maximum(slack, 0))
    moved = jax.random.randint(jax.random.fold_in(own, 4), (amount // 2,), 0, 1 << 20) % (slack + 1)
    tallies = tallies.at[donor].add(-moved).at[receiver].add(moved)
    labels = jnp.searchsorted(jnp.cumsum(tallies), jnp.arange(rows * top), side="right").astype(jnp.int32)
    grid = labels.reshape(top, rows).T
    grid = grid[jax.random.permutation(jax.random.fold_in(own, 1), rows)]
    rotation = jax.random.randint(jax.random.fold_in(own, 2), (rows, 1), 0, top)
    return jnp.take_along_axis(grid, (jnp.arange(top)[None, :] + rotation) % top, axis=1)


def portions_of(number_of, total, bound, skew, full):
    weights = [(1 << 20) // math.isqrt(standing ** skew) + 1 for standing in range(1, number_of + 1)]
    largest = bound if full else min(bound, max(-(-total // number_of), total * weights[0] // sum(weights)))
    least = 1 if total - largest >= number_of - 1 else 0
    holding, spare = [largest] + [least] * (number_of - 1), total - largest - least * (number_of - 1)
    while spare > 0:
        movable = [i for i in range(1, number_of) if holding[i] < largest] or [i for i in range(1, number_of) if holding[i] < bound]
        mass, left = sum([weights[i] for i in movable]), spare
        for i in movable:
            addition = min(bound - holding[i], max(1, left * weights[i] // mass), spare)
            holding[i] = holding[i] + addition
            spare = spare - addition
    return np.array(holding)


def noise(stream_key, shape, scale, reach, cuts=(), held_as=jnp.bfloat16):
    result = jax.random.normal(stream_key, shape, jnp.float32) * scale
    if len(cuts) > 0:
        result = levels(stream_key, shape, cuts, -0.22, 0.18) * result
    return jnp.clip(result, min=-reach, max=reach).astype(held_as)


def setup_inputs(seed: int = 0) -> dict:
    splits = jax.random.split(jax.random.key(seed), 5)
    tokens = noise(splits[0], (TOKENS, D), 1.0, 6.0, ((0, 128), (1, 8)))
    expert_ids_keys = jax.random.split(jax.random.fold_in(splits[1], 1), TOKENS // TOK_DEV)
    expert_ids_turns = jax.random.permutation(jax.random.fold_in(splits[1], 3), TOKENS // TOK_DEV)
    expert_ids = jax.vmap(lambda own, number: assign_block(jax.random.fold_in(splits[1], 2), own, number, TOK_DEV, EXPERTS, 2, CAP, 1))(expert_ids_keys, expert_ids_turns).reshape((TOKENS, 2))
    weights = noise(splits[2], (EXPERTS, D, FF), D ** -0.5, 0.109375, ((0, 8), (2, 8)))
    cotangent = noise(splits[3], (GROUPS, EXPERTS, SLOTS, FF), 1.0, 6.0, ((0, 16), (1, 8), (3, 8)))
    return dict(tokens=tokens, expert_ids=expert_ids, weights=weights, cotangent=cotangent)


def route_slots(routed):
    onehot = (routed[:, None] == jnp.arange(EXPERTS, dtype=jnp.int32)[None, :]).astype(jnp.int32)
    before = jnp.cumsum(onehot, axis=0) - onehot
    return (routed * CAP + jnp.sum(before * onehot, axis=1)).astype(jnp.int32)


def per_expert(pack):
    expert_rows, expert_weight, expert_cot = pack
    rows = expert_rows.reshape(N_DP * SLOTS, D)
    preact = jnp.dot(rows, expert_weight, preferred_element_type=jnp.float32)
    gate_sig = jax.nn.sigmoid(preact)
    hidden = (preact * gate_sig).astype(jnp.bfloat16)
    slope = (expert_cot.reshape(N_DP * SLOTS, FF).astype(jnp.float32) * gate_sig * (1.0 + preact * (1.0 - gate_sig))).astype(jnp.bfloat16)

    def add_group(total, pair):
        rows_group, slope_group = pair
        term = lax.dot_general(rows_group, slope_group, (((0,), (0,)), ((), ())), preferred_element_type=jnp.float32)
        return total + term.astype(jnp.bfloat16).astype(jnp.float32), None

    grad, _ = lax.scan(add_group, jnp.zeros((D, FF), jnp.float32), (expert_rows, slope.reshape(N_DP, SLOTS, FF)))
    width = FF // N_TP
    slope_parts = slope.reshape(N_DP * SLOTS, N_TP, width).transpose(1, 0, 2)
    weight_parts = expert_weight.reshape(D, N_TP, width).transpose(1, 0, 2)

    def add_shard(total, pair):
        slope_block, weight_block = pair
        term = lax.dot_general(slope_block, weight_block, (((1,), (1,)), ((), ())), preferred_element_type=jnp.float32)
        return total + term.astype(jnp.bfloat16).astype(jnp.float32), None

    back, _ = lax.scan(add_shard, jnp.zeros((N_DP * SLOTS, D), jnp.float32), (slope_parts, weight_parts))
    return hidden.reshape(N_DP, SLOTS, FF), grad.astype(jnp.bfloat16), back.astype(jnp.bfloat16).reshape(N_DP, SLOTS, D)


def reference(tokens, expert_ids, weights, cotangent):
    blocks = N_DP * N_CTX
    routed = expert_ids.reshape(blocks, 2 * TOK_DEV).astype(jnp.int32)
    target = jax.vmap(route_slots)(routed)
    route_rows = jnp.repeat(tokens.reshape(blocks, TOK_DEV, D), 2, axis=1)
    block_index = jnp.arange(blocks, dtype=jnp.int32)[:, None] * jnp.ones((1, 2 * TOK_DEV), jnp.int32)
    buffer = jnp.zeros((blocks, EXPERTS * CAP, D), jnp.bfloat16).at[block_index, target].set(route_rows)
    slots = buffer.reshape(N_DP, N_CTX, EXPERTS, CAP, D).transpose(0, 2, 1, 3, 4).reshape(N_DP, EXPERTS, SLOTS, D)
    hidden_all, grads, backs = lax.map(per_expert, (slots.transpose(1, 0, 2, 3), weights, cotangent.transpose(1, 0, 2, 3)))
    hidden = hidden_all.transpose(1, 0, 2, 3)
    back_slots = backs.transpose(1, 0, 2, 3).reshape(N_DP, EXPERTS, N_CTX, CAP, D).transpose(0, 2, 1, 3, 4).reshape(blocks, EXPERTS * CAP, D)
    picked = jnp.take_along_axis(back_slots, target[:, :, None], axis=1)
    token_grad = picked.astype(jnp.float32).reshape(blocks, TOK_DEV, 2, D).sum(axis=2).astype(jnp.bfloat16).reshape(TOKENS, D)
    return hidden, grads, token_grad
```

```python
import functools

import jax
import jax.numpy as jnp
from jax import lax
from jax.experimental import pallas as pl
from jax.experimental.pallas import tpu as pltpu
from jax.sharding import PartitionSpec as P

MESH = pl.DeviceIdType.MESH
BF16 = jnp.bfloat16
F32 = jnp.float32
HI = 2
CORES = 2
PARTS = 4


def xor(a, bits):
    for bit in (1, 2, 4, 8):
        if bits & bit:
            a = a + bit - 2 * bit * ((a // bit) % 2)
    return a


def nt(a, b):
    return lax.dot_general(a, b, (((1,), (1,)), ((), ())), preferred_element_type=F32)


def tn(a, b):
    return lax.dot_general(a, b, (((0,), (0,)), ((), ())), preferred_element_type=F32)


def nn(a, b):
    return jnp.dot(a, b, preferred_element_type=F32)


def kernel(
    dims,
    tokens, place, place_t, pack, unpack, w_hbm, cot,
    hidden, wgrad, tgrad,
    w, ysend, yrecv, g, r, acc, s, psend, precv, qsend, t, hsend, hrecv, wsend, wkeep, wrecv,
    w_sem, y_ss, y_rs, gd_ss, gd_rs, gf_ss, gf_rs, r_ss, rf_ss, r_rs, s_ss, s_rs,
    p_ss, p_rs, t_ss, t_rs, h_ss, h_rs, x_ss, x_rs,
):
    n_z, n_ctx, n_lo = dims
    feat = tokens.shape[1]
    cols = cot.shape[1] // PARTS
    half = feat // HI
    dp, e, j = lax.axis_index("dp"), lax.axis_index("ctx"), lax.axis_index("tp")
    z, hi = dp // HI, dp % HI
    lo, core = j // CORES, j % CORES
    waits = []

    def copy(src, dst, ssem, rsem, to):
        return pltpu.make_async_remote_copy(
            src_ref=src, dst_ref=dst, send_sem=ssem, recv_sem=rsem,
            device_id=to, device_id_type=MESH,
        )

    def send(*args):
        made = copy(*args)
        made.start()
        waits.append(made)

    def on_y(d):
        return (dp, (e + d) % n_ctx, j)

    def on_z(k):
        return (k * HI + hi, e, j)

    def on_lo(o):
        return (dp, e, xor(lo, o) * CORES + core)

    other = (dp, e, lo * CORES + 1 - core)
    across = (z * HI + 1 - hi, e, j)

    w_copy = pltpu.make_async_copy(w_hbm, w, w_sem)
    w_copy.start()

    partners = [on_y(d) for d in range(1, n_ctx)]
    partners += [on_z((z + d) % n_z) for d in range(1, n_z)]
    partners += [on_lo(o) for o in range(1, n_lo)]
    partners += [other, across]
    barrier = pltpu.get_barrier_semaphore()
    for to in partners:
        pl.semaphore_signal(barrier, inc=1, device_id=to, device_id_type=MESH)

    ysend[...] = nn(place[...], tokens[...]).astype(BF16).reshape(ysend.shape)
    pl.semaphore_wait(barrier, len(partners))

    far = sorted(range(1, n_ctx), key=lambda d: -min(d, n_ctx - d))
    for d in far:
        send(ysend.at[(e + d) % n_ctx], yrecv.at[e], y_ss.at[d - 1], y_rs.at[d - 1], on_y(d))
    yrecv[e] = ysend[e]
    for d in far:
        copy(ysend.at[0], yrecv.at[(e - d + n_ctx) % n_ctx], y_ss.at[d - 1], y_rs.at[d - 1], on_y(d)).wait_recv()
    g[j] = nn(pack[...], yrecv[...].reshape(-1, feat)).astype(BF16)

    for o in range(1, n_lo):
        send(g.at[j], g.at[j], gd_ss.at[o], gd_rs.at[o], on_lo(o))
    send(g.at[j], g.at[j], gf_ss.at[0], gf_rs.at[0], other)

    def rows_copy(o):
        k = xor(lo, o) * CORES + core
        return k, copy(g.at[k], r.at[z], r_ss.at[o], r_rs.at[z], on_z(k))

    def rows_start(o):
        k, made = rows_copy(o)

        @pl.when(k != z)
        def _():
            made.start()

    def project(k, first=False):
        @pl.loop(0, PARTS)
        def _(q):
            at = pl.ds(pl.multiple_of(q * cols, cols), cols)
            term = nn(g[k], w[pl.ds(pl.multiple_of(k * feat, feat), feat), at])
            acc[q] = term if first else acc[q] + term

    rows_start(0)
    w_copy.wait()
    project(j, True)
    k = lo * CORES + 1 - core
    copy(g.at[j], g.at[k], gf_ss.at[0], gf_rs.at[0], other).wait_recv()
    project(k)
    for o in range(1, n_lo):
        k = xor(lo, o) * CORES + core
        copy(g.at[j], g.at[k], gd_ss.at[o], gd_rs.at[o], on_lo(o)).wait_recv()
        send(g.at[k], g.at[k], gf_ss.at[o], gf_rs.at[o], other)
        rows_start(o)
        project(k)
    for o in range(1, n_lo):
        k = xor(lo, o) * CORES + 1 - core
        copy(g.at[j], g.at[k], gf_ss.at[o], gf_rs.at[o], other).wait_recv()
        project(k)

    def reach(way, q):
        return n_z // 2 if q % 2 == way else n_z - 1 - n_z // 2

    def step_to(way):
        return on_z((z + 1) % n_z if way == 0 else (z + n_z - 1) % n_z)

    def own(q):
        for way in (0, 1):
            send(s.at[q, z], s.at[q, z], s_ss.at[way, q, 0], s_rs.at[way, q, 0], step_to(way))

    def step(q, d):
        for way in (0, 1):
            if d <= reach(way, q):
                src = (z - d + n_z) % n_z if way == 0 else (z + d) % n_z
                copy(s.at[q, z], s.at[q, src], s_ss.at[way, q, d - 1], s_rs.at[way, q, d - 1], step_to(way)).wait_recv()
                if d < reach(way, q):
                    send(s.at[q, src], s.at[q, src], s_ss.at[way, q, d], s_rs.at[way, q, d], step_to(way))

    for q in range(PARTS):
        at = slice(q * cols, (q + 1) * cols)
        p = acc[q]
        gate = jax.nn.sigmoid(p)
        hidden[:, at] = (p * gate).astype(BF16)
        s[q, z] = (cot[:, at].astype(F32) * gate * (1.0 + p * (1.0 - gate))).astype(BF16)
        if q < 2:
            own(q)

    def back(k):
        rows = pl.ds(pl.multiple_of(k * feat, feat), feat)
        total = nt(s[0, z], w[rows, 0:cols])
        for q in range(1, PARTS):
            total = total + nt(s[q, z], w[rows, q * cols:(q + 1) * cols])
        return total

    for m in range(n_lo):
        psend[m] = back(m * CORES + 1 - core).astype(BF16)
        send(psend.at[m], precv.at[m], p_ss.at[m], p_rs.at[m], other)

    for d in (1,):
        step(0, d), step(1, d)

    for m in range(n_lo):
        copy(psend.at[m], precv.at[m], p_ss.at[m], p_rs.at[m], other).wait_recv()
    for o in (*range(1, n_lo), 0):
        m = xor(lo, o)
        qsend[o] = (back(m * CORES + core) + precv[m].astype(F32)).astype(BF16)
        if o:
            send(qsend.at[o], t.at[o], t_ss.at[o], t_rs.at[o], on_lo(o))

    for d in range(2, n_z // 2):
        step(0, d), step(1, d)
        if d == 2:
            own(2), own(3)
    if n_z // 2 <= 2:
        own(2), own(3)

    r[z] = g[z]
    for d in range(1, n_z):
        src = (z + d) % n_z
        copy(g.at[0], r.at[src], rf_ss.at[d - 1], r_rs.at[src], other).wait_recv()

        @pl.when(core == z % CORES)
        def _():
            copy(r.at[src], r.at[src], rf_ss.at[d - 1], r_rs.at[src], other).start()

    step(0, n_z // 2), step(1, n_z // 2)
    step(2, 1), step(3, 1)

    def product(q):
        right = s[q].reshape(-1, cols)
        whole = tn(r[...].reshape(-1, feat), right)
        wkeep[q] = whole
        theirs = wkeep[q, pl.ds(pl.multiple_of((1 - hi) * half, half), half), :]
        wsend[q] = theirs.astype(BF16)
        send(wsend.at[q], wrecv.at[q], x_ss.at[q], x_rs.at[q], across)

    product(0)
    product(1)
    step(2, 2), step(3, 2)

    summed = qsend[0].astype(F32)
    for o in range(1, n_lo):
        copy(qsend.at[o], t.at[o], t_ss.at[o], t_rs.at[o], on_lo(o)).wait_recv()
        summed = summed + t[o].astype(F32)
    hsend[...] = nn(unpack[...], summed.astype(BF16)).astype(BF16).reshape(hsend.shape)
    for d in far:
        send(hsend.at[(e + d) % n_ctx], hrecv.at[e], h_ss.at[d - 1], h_rs.at[d - 1], on_y(d))
    hrecv[e] = hsend[e]

    for d in range(3, n_z // 2 + 1):
        step(2, d), step(3, d)
    product(2)
    product(3)

    for d in far:
        copy(hsend.at[0], hrecv.at[(e - d + n_ctx) % n_ctx], h_ss.at[d - 1], h_rs.at[d - 1], on_y(d)).wait_recv()
    tgrad[...] = nn(place_t[...], hrecv[...].reshape(-1, feat)).astype(BF16)

    for q in range(PARTS):
        copy(wsend.at[q], wrecv.at[q], x_ss.at[q], x_rs.at[q], across).wait_recv()
        mine = wkeep[q, pl.ds(pl.multiple_of(hi * half, half), half), :]
        wgrad[:, q * cols:(q + 1) * cols] = (mine + wrecv[q].astype(F32)).astype(BF16)

    for made in waits:
        made.wait_send()
    for o in range(n_lo):
        k, made = rows_copy(o)

        @pl.when(k != z)
        def _():
            made.wait_send()

    @pl.when(core == z % CORES)
    def _():
        for d in range(1, n_z):
            src = (z + d) % n_z
            copy(r.at[src], r.at[src], rf_ss.at[d - 1], r_rs.at[src], other).wait_send()


def per_device(tokens, expert_ids, weights, cotangent):
    n_ctx, n_tp, n_dp = lax.axis_size("ctx"), lax.axis_size("tp"), lax.axis_size("dp")
    n_z, n_lo = n_dp // HI, n_tp // CORES
    count, feat = tokens.shape
    slots, ff = cotangent.shape[2:]
    capacity = slots // n_ctx
    padded = -(-capacity // 16) * 16
    cols, half = ff // PARTS, feat // HI

    routed = expert_ids.reshape(-1)
    onehot = (routed[:, None] == jnp.arange(n_ctx, dtype=jnp.int32)[None, :]).astype(jnp.int32)
    before = jnp.cumsum(onehot, axis=0) - onehot
    target = (routed * padded + jnp.sum(before * onehot, axis=1)).reshape(count, 2)
    places = jnp.arange(n_ctx * padded, dtype=jnp.int32)
    place = ((places[:, None] == target[None, :, 0]) | (places[:, None] == target[None, :, 1])).astype(BF16)
    place_t = ((places[None, :] == target[:, :1]) | (places[None, :] == target[:, 1:])).astype(BF16)
    slot = jnp.arange(slots, dtype=jnp.int32)
    spread = slot // capacity * padded + slot % capacity
    pack = (spread[:, None] == places[None, :]).astype(BF16)
    unpack = (places[:, None] == spread[None, :]).astype(BF16)

    vmem = pl.BlockSpec(memory_space=pltpu.VMEM)
    dma = pltpu.SemaphoreType.DMA
    hidden, wgrad, tgrad = pl.pallas_call(
        functools.partial(kernel, (n_z, n_ctx, n_lo)),
        out_shape=(
            jax.ShapeDtypeStruct((slots, ff), BF16),
            jax.ShapeDtypeStruct((half, ff), BF16),
            jax.ShapeDtypeStruct((count, feat), BF16),
        ),
        in_specs=[vmem] * 5 + [pl.BlockSpec(memory_space=pl.ANY), vmem],
        out_specs=(vmem, vmem, vmem),
        scratch_shapes=[
            pltpu.VMEM(weights.shape[1:], BF16),
            pltpu.VMEM((n_ctx, padded, feat), BF16),
            pltpu.VMEM((n_ctx, padded, feat), BF16),
            pltpu.VMEM((n_tp, slots, feat), BF16),
            pltpu.VMEM((n_z, slots, feat), BF16),
            pltpu.VMEM((PARTS, slots, cols), F32),
            pltpu.VMEM((PARTS, n_z, slots, cols), BF16),
            pltpu.VMEM((n_lo, slots, feat), BF16),
            pltpu.VMEM((n_lo, slots, feat), BF16),
            pltpu.VMEM((n_lo, slots, feat), BF16),
            pltpu.VMEM((n_lo, slots, feat), BF16),
            pltpu.VMEM((n_ctx, padded, feat), BF16),
            pltpu.VMEM((n_ctx, padded, feat), BF16),
            pltpu.VMEM((PARTS, half, cols), BF16),
            pltpu.VMEM((PARTS, feat, cols), F32),
            pltpu.VMEM((PARTS, half, cols), BF16),
            dma,
            dma((n_ctx - 1,)), dma((n_ctx - 1,)),
            dma((n_lo,)), dma((n_lo,)),
            dma((n_lo,)), dma((n_lo,)),
            dma((n_lo,)), dma((n_z - 1,)), dma((n_z,)),
            dma((2, PARTS, n_z // 2)), dma((2, PARTS, n_z // 2)),
            dma((n_lo,)), dma((n_lo,)),
            dma((n_lo,)), dma((n_lo,)),
            dma((n_ctx - 1,)), dma((n_ctx - 1,)),
            dma((PARTS,)), dma((PARTS,)),
        ],
        compiler_params=pltpu.CompilerParams(
            collective_id=0, has_side_effects=True, vmem_limit_bytes=48 * 1024 * 1024
        ),
    )(tokens, place, place_t, pack, unpack, weights[0], cotangent[0, 0])
    return hidden[None, None], wgrad[None], tgrad


def solution(mesh):
    placed = (
        P(("dp", "ctx"), "tp"),
        P(("dp", "ctx"), None),
        P("ctx", None, "tp"),
        P("dp", "ctx", None, "tp"),
    )
    return jax.shard_map(
        per_device,
        mesh=mesh,
        in_specs=placed,
        out_specs=(P("dp", "ctx", None, "tp"), P("ctx", "dp", "tp"), P(("dp", "ctx"), "tp")),
        check_vma=False,
    )
```

```python
import functools

import jax
import jax.numpy as jnp
from jax import lax
from jax.experimental import pallas as pl
from jax.experimental.pallas import tpu as pltpu
from jax.sharding import PartitionSpec as P

MESH = pl.DeviceIdType.MESH
BF16 = jnp.bfloat16
F32 = jnp.float32
HI = 2
CORES = 2
ROWS = 16
LANES = 128
PARTS = 4


def xor(a, bits):
    for bit in (1, 2, 4, 8):
        if bits & bit:
            a = a + bit - 2 * bit * ((a // bit) % 2)
    return a


def nt(a, b):
    return lax.dot_general(a, b, (((1,), (1,)), ((), ())), preferred_element_type=F32)


def tn(a, b):
    return lax.dot_general(a, b, (((0,), (0,)), ((), ())), preferred_element_type=F32)


def nn(a, b):
    return jnp.dot(a, b, preferred_element_type=F32)


def kernel(
    dims,
    tokens_hbm, ids_hbm, w_hbm, cot_hbm,
    hidden_hbm, wgrad_hbm, tgrad_hbm,
    hidden, wgrad, tgrad, tokens, ids, cot, place, rt, w, ysend, yrecv, g, r, acc, s, psend, precv, qsend, t, hsend, hrecv, wsend, wkeep, wrecv,
    in_sems, out_sems, y_ss, y_rs, gd_ss, gd_rs, gf_ss, gf_rs, r_ss, rf_ss, r_rs, s_ss, s_rs,
    p_ss, p_rs, t_ss, t_rs, h_ss, h_rs, x_ss, x_rs,
):
    n_z, n_ctx, n_lo, capacity = dims
    feat = tokens.shape[1]
    slots = cot.shape[0]
    cols = cot.shape[1] // PARTS
    half = feat // HI
    dp, e, j = lax.axis_index("dp"), lax.axis_index("ctx"), lax.axis_index("tp")
    z, hi = dp // HI, dp % HI
    lo, core = j // CORES, j % CORES
    waits = []

    def copy(src, dst, ssem, rsem, to):
        return pltpu.make_async_remote_copy(
            src_ref=src, dst_ref=dst, send_sem=ssem, recv_sem=rsem,
            device_id=to, device_id_type=MESH,
        )

    def send(*args):
        made = copy(*args)
        made.start()
        waits.append(made)

    stores = []

    def store(src, dst):
        made = pltpu.make_async_copy(src, dst, out_sems.at[len(stores)])
        made.start()
        stores.append(made)

    def on_y(d):
        return (dp, (e + d) % n_ctx, j)

    def on_z(k):
        return (k * HI + hi, e, j)

    def on_lo(o):
        return (dp, e, xor(lo, o) * CORES + core)

    other = (dp, e, lo * CORES + 1 - core)
    across = (z * HI + 1 - hi, e, j)

    loads = [
        pltpu.make_async_copy(src, dst, in_sems.at[i])
        for i, (src, dst) in enumerate(((ids_hbm, ids), (tokens_hbm, tokens), (cot_hbm, cot), (w_hbm, w)))
    ]
    for load in loads:
        load.start()

    partners = [on_y(d) for d in range(1, n_ctx)]
    partners += [on_z((z + d) % n_z) for d in range(1, n_z)]
    partners += [on_lo(o) for o in range(1, n_lo)]
    partners += [other, across]
    barrier = pltpu.get_barrier_semaphore()
    for to in partners:
        pl.semaphore_signal(barrier, inc=1, device_id=to, device_id_type=MESH)

    count, folds = tokens.shape[0], feat // LANES
    beyond = (capacity - ROWS) * folds
    loads[0].wait()
    name = lax.broadcasted_iota(jnp.int32, (n_ctx, count), 0)
    named = ((ids[0:1, :] == name) | (ids[1:2, :] == name)).astype(F32)
    earlier = lax.broadcasted_iota(jnp.int32, (count, count), 0) < lax.broadcasted_iota(jnp.int32, (count, count), 1)
    rank = jnp.where(named > 0.0, nn(named.astype(BF16), earlier.astype(F32).astype(BF16)), -1.0)

    def slot_of(row, kind):
        if kind == 0:
            return row
        slot = jnp.full_like(row, -2)
        for r in range(kind - 1, beyond, folds):
            slot = jnp.where(row == r, ROWS + r // folds, slot)
        return slot

    row = lax.broadcasted_iota(jnp.int32, (ROWS, count), 0)
    for kind in range(folds + 1):
        slot = slot_of(row, kind).astype(F32)
        for x in range(n_ctx):
            place[kind, x * ROWS:(x + 1) * ROWS, :] = (rank[x:x + 1, :] == slot).astype(F32).astype(BF16)

    def fold(mats, rows):
        wide = nn(mats[0], rows)
        tail = nn(mats[1], rows[:, 0:LANES])
        for f in range(1, folds):
            tail = tail + nn(mats[f + 1], rows[:, f * LANES:(f + 1) * LANES])
        return jnp.concatenate([wide, tail], axis=1).astype(BF16).reshape(ysend.shape)

    def unfold(mats, blocks, dot):
        wide = dot(mats[0], blocks[:, 0:feat])
        tail = blocks[:, feat:]
        return wide + jnp.concatenate([dot(mats[f + 1], tail) for f in range(folds)], axis=1)

    loads[1].wait()
    ysend[...] = fold(place, tokens[...])
    pl.semaphore_wait(barrier, len(partners))

    def spread(kind, rows_at):
        shape = [slots, n_ctx * ROWS] if rows_at == 0 else [n_ctx * ROWS, slots]
        want, col = lax.broadcasted_iota(jnp.int32, shape, rows_at), lax.broadcasted_iota(jnp.int32, shape, 1 - rows_at)
        within = slot_of(col & (ROWS - 1), kind)
        same = ((col >> (ROWS.bit_length() - 1)) * capacity + within == want) & (within >= 0)
        return same.astype(F32).astype(BF16)

    far = sorted(range(1, n_ctx), key=lambda d: -min(d, n_ctx - d))
    for d in far:
        send(ysend.at[(e + d) % n_ctx], yrecv.at[e], y_ss.at[d - 1], y_rs.at[d - 1], on_y(d))
    yrecv[e] = ysend[e]
    pack = [spread(kind, 0) for kind in range(folds + 1)]
    for d in far:
        copy(ysend.at[0], yrecv.at[(e - d + n_ctx) % n_ctx], y_ss.at[d - 1], y_rs.at[d - 1], on_y(d)).wait_recv()
    g[j] = unfold(pack, yrecv[...].reshape(-1, feat + LANES), nn).astype(BF16)

    near = [o for o in (2, 1) if o < n_lo]
    inner = (lo + 1) // 2 % 2 == 1
    end = 3
    direct = copy(g.at[j], g.at[j], gd_ss.at[n_lo - 1], gd_rs.at[n_lo - 1], on_lo(n_lo - 1))
    passed = xor(lo, n_lo // 2) * CORES + core
    through = copy(g.at[passed], g.at[passed], gd_ss.at[0], gd_rs.at[n_lo - 1], on_lo(1))
    send(g.at[j], g.at[j], gd_ss.at[near[0]], gd_rs.at[near[0]], on_lo(near[0]))
    if n_lo > end:

        @pl.when(inner)
        def _():
            direct.start()

    send(g.at[j], g.at[j], gf_ss.at[0], gf_rs.at[0], other)
    for o in near[1:]:
        send(g.at[j], g.at[j], gd_ss.at[o], gd_rs.at[o], on_lo(o))

    def rows_copy(o):
        k = xor(lo, o) * CORES + core
        return k, copy(g.at[k], r.at[z], r_ss.at[o], r_rs.at[z], on_z(k))

    def rows_start(o):
        k, made = rows_copy(o)

        @pl.when(k != z)
        def _():
            made.start()

    def project(k, first=False):
        @pl.loop(0, PARTS)
        def _(q):
            at = pl.ds(pl.multiple_of(q * cols, cols), cols)
            term = nn(g[k], w[pl.ds(pl.multiple_of(k * feat, feat), feat), at])
            acc[q] = term if first else acc[q] + term

    rows_start(0)
    loads[3].wait()
    project(j, True)
    k = lo * CORES + 1 - core
    copy(g.at[j], g.at[k], gf_ss.at[0], gf_rs.at[0], other).wait_recv()
    project(k)
    order = near + [end] * (n_lo > end)
    for o in order:
        k = xor(lo, o) * CORES + core
        copy(g.at[j], g.at[k], gd_ss.at[o], gd_rs.at[o], on_lo(o)).wait_recv()
        if n_lo > end and o == near[0]:

            @pl.when(inner)
            def _():
                through.start()

        send(g.at[k], g.at[k], gf_ss.at[o], gf_rs.at[o], other)
        rows_start(o)
        project(k)
    for o in order:
        k = xor(lo, o) * CORES + 1 - core
        copy(g.at[j], g.at[k], gf_ss.at[o], gf_rs.at[o], other).wait_recv()
        if o != order[-1]:
            project(k)
    last = k

    def reach(way, q):
        return n_z // 2 if q % 2 == way else n_z - 1 - n_z // 2

    def step_to(way):
        return on_z((z + 1) % n_z if way == 0 else (z + n_z - 1) % n_z)

    def own(q):
        for way in (0, 1):
            send(s.at[q, z], s.at[q, z], s_ss.at[way, q, 0], s_rs.at[way, q, 0], step_to(way))

    def step(q, d):
        for way in (0, 1):
            if d <= reach(way, q):
                src = (z - d + n_z) % n_z if way == 0 else (z + d) % n_z
                copy(s.at[q, z], s.at[q, src], s_ss.at[way, q, d - 1], s_rs.at[way, q, d - 1], step_to(way)).wait_recv()
                if d < reach(way, q):
                    send(s.at[q, src], s.at[q, src], s_ss.at[way, q, d], s_rs.at[way, q, d], step_to(way))

    loads[2].wait()
    for q in range(PARTS):
        at = slice(q * cols, (q + 1) * cols)
        p = acc[q] + nn(g[last], w[pl.ds(pl.multiple_of(last * feat, feat), feat), at])
        acc[q] = p
        gate = jax.nn.sigmoid(p)
        s[q, z] = (cot[:, at].astype(F32) * gate * (1.0 + p * (1.0 - gate))).astype(BF16)
        own(q)

    def back(k):
        rows = pl.ds(pl.multiple_of(k * feat, feat), feat)
        total = nt(s[0, z], w[rows, 0:cols])
        for q in range(1, PARTS):
            total = total + nt(s[q, z], w[rows, q * cols:(q + 1) * cols])
        return total

    for m in range(n_lo):
        psend[m] = back(m * CORES + 1 - core).astype(BF16)
        send(psend.at[m], precv.at[m], p_ss.at[m], p_rs.at[m], other)

    first, second = (0, 1), (2, 3)
    n_d = n_z // 2

    def steps(part, d):
        for q in part:
            step(q, d)

    steps(first, 1)

    for m in range(n_lo):
        copy(psend.at[m], precv.at[m], p_ss.at[m], p_rs.at[m], other).wait_recv()
    for o in (*range(1, n_lo), 0):
        m = xor(lo, o)
        qsend[o] = (back(m * CORES + core) + precv[m].astype(F32)).astype(BF16)
        if o:
            send(qsend.at[o], t.at[o], t_ss.at[o], t_rs.at[o], on_lo(o))

    if n_d > 2:
        steps(first, 2)
    steps(second, 1)

    r[z] = g[z]
    for d in range(1, n_z):
        src = (z + d) % n_z
        copy(g.at[0], r.at[src], rf_ss.at[d - 1], r_rs.at[src], other).wait_recv()

        @pl.when(core == z % CORES)
        def _():
            copy(r.at[src], r.at[src], rf_ss.at[d - 1], r_rs.at[src], other).start()

    for d in range(3, n_d):
        steps(first, d)
        steps(second, d - 1)

    rt[...] = r[...].reshape(-1, feat).T
    for q in range(PARTS):
        p = acc[q]
        hidden[:, q * cols:(q + 1) * cols] = (p * jax.nn.sigmoid(p)).astype(BF16)
    store(hidden, hidden_hbm)

    def product(q, side):
        return nn(rt[pl.ds(pl.multiple_of(side * half, half), half), :], s[q].reshape(-1, cols))

    def theirs(q):
        wsend[q] = product(q, 1 - hi).astype(BF16)
        send(wsend.at[q], wrecv.at[q], x_ss.at[q], x_rs.at[q], across)

    steps(first, n_d)
    for q in first:
        theirs(q)
    if n_d > 2:
        steps(second, n_d - 1)

    summed = qsend[0].astype(F32)
    for o in range(1, n_lo):
        copy(qsend.at[o], t.at[o], t_ss.at[o], t_rs.at[o], on_lo(o)).wait_recv()
        summed = summed + t[o].astype(F32)
    hsend[...] = fold([spread(kind, 1) for kind in range(folds + 1)], summed.astype(BF16))
    for d in far:
        send(hsend.at[(e + d) % n_ctx], hrecv.at[e], h_ss.at[d - 1], h_rs.at[d - 1], on_y(d))
    hrecv[e] = hsend[e]

    for q in first:
        wkeep[q] = product(q, hi)
    steps(second, n_d)
    for q in second:
        theirs(q)
    for q in second:
        wkeep[q] = product(q, hi)

    for d in far:
        copy(hsend.at[0], hrecv.at[(e - d + n_ctx) % n_ctx], h_ss.at[d - 1], h_rs.at[d - 1], on_y(d)).wait_recv()
    tgrad[...] = unfold(place, hrecv[...].reshape(-1, feat + LANES), tn).astype(BF16)
    store(tgrad, tgrad_hbm)

    for q in range(PARTS):
        copy(wsend.at[q], wrecv.at[q], x_ss.at[q], x_rs.at[q], across).wait_recv()
        at = slice(q * cols, (q + 1) * cols)
        wgrad[:, at] = (wkeep[q] + wrecv[q].astype(F32)).astype(BF16)
        store(wgrad.at[:, at], wgrad_hbm.at[:, at])

    for made in waits:
        made.wait_send()
    for made in stores:
        made.wait()
    if n_lo > end:

        @pl.when(inner)
        def _():
            direct.wait_send()
            through.wait_send()
    for o in range(n_lo):
        k, made = rows_copy(o)

        @pl.when(k != z)
        def _():
            made.wait_send()

    @pl.when(core == z % CORES)
    def _():
        for d in range(1, n_z):
            src = (z + d) % n_z
            copy(r.at[src], r.at[src], rf_ss.at[d - 1], r_rs.at[src], other).wait_send()


def per_device(tokens, expert_ids, weights, cotangent):
    n_ctx, n_tp, n_dp = lax.axis_size("ctx"), lax.axis_size("tp"), lax.axis_size("dp")
    n_z, n_lo = n_dp // HI, n_tp // CORES
    count, feat = tokens.shape
    slots, ff = cotangent.shape[2:]
    capacity = slots // n_ctx
    cols, half = ff // PARTS, feat // HI

    dma = pltpu.SemaphoreType.DMA
    hidden, wgrad, tgrad = pl.pallas_call(
        functools.partial(kernel, (n_z, n_ctx, n_lo, capacity)),
        out_shape=(
            jax.ShapeDtypeStruct((slots, ff), BF16),
            jax.ShapeDtypeStruct((half, ff), BF16),
            jax.ShapeDtypeStruct((count, feat), BF16),
        ),
        in_specs=[pl.BlockSpec(memory_space=pl.ANY)] * 4,
        out_specs=[pl.BlockSpec(memory_space=pl.ANY)] * 3,
        scratch_shapes=[
            pltpu.VMEM((slots, ff), BF16),
            pltpu.VMEM((half, ff), BF16),
            pltpu.VMEM((count, feat), BF16),
            pltpu.VMEM((count, feat), BF16),
            pltpu.VMEM((2, count), jnp.int32),
            pltpu.VMEM((slots, ff), BF16),
            pltpu.VMEM((feat // LANES + 1, n_ctx * ROWS, count), BF16),
            pltpu.VMEM((feat, n_z * slots), BF16),
            pltpu.VMEM(weights.shape[1:], BF16),
            pltpu.VMEM((n_ctx, ROWS, feat + LANES), BF16),
            pltpu.VMEM((n_ctx, ROWS, feat + LANES), BF16),
            pltpu.VMEM((n_tp, slots, feat), BF16),
            pltpu.VMEM((n_z, slots, feat), BF16),
            pltpu.VMEM((PARTS, slots, cols), F32),
            pltpu.VMEM((PARTS, n_z, slots, cols), BF16),
            pltpu.VMEM((n_lo, slots, feat), BF16),
            pltpu.VMEM((n_lo, slots, feat), BF16),
            pltpu.VMEM((n_lo, slots, feat), BF16),
            pltpu.VMEM((n_lo, slots, feat), BF16),
            pltpu.VMEM((n_ctx, ROWS, feat + LANES), BF16),
            pltpu.VMEM((n_ctx, ROWS, feat + LANES), BF16),
            pltpu.VMEM((PARTS, half, cols), BF16),
            pltpu.VMEM((PARTS, half, cols), F32),
            pltpu.VMEM((PARTS, half, cols), BF16),
            dma((4,)), dma((2 + PARTS,)),
            dma((n_ctx - 1,)), dma((n_ctx - 1,)),
            dma((n_lo,)), dma((n_lo,)),
            dma((n_lo,)), dma((n_lo,)),
            dma((n_lo,)), dma((n_z - 1,)), dma((n_z,)),
            dma((2, PARTS, n_z // 2)), dma((2, PARTS, n_z // 2)),
            dma((n_lo,)), dma((n_lo,)),
            dma((n_lo,)), dma((n_lo,)),
            dma((n_ctx - 1,)), dma((n_ctx - 1,)),
            dma((PARTS,)), dma((PARTS,)),
        ],
        compiler_params=pltpu.CompilerParams(
            collective_id=0, has_side_effects=True, vmem_limit_bytes=48 * 1024 * 1024
        ),
    )(tokens, expert_ids.T, weights[0], cotangent[0, 0])
    return hidden[None, None], wgrad[None], tgrad


def solution(mesh):
    placed = (
        P(("dp", "ctx"), "tp"),
        P(("dp", "ctx"), None),
        P("ctx", None, "tp"),
        P("dp", "ctx", None, "tp"),
    )
    return jax.shard_map(
        per_device,
        mesh=mesh,
        in_specs=placed,
        out_specs=(P("dp", "ctx", None, "tp"), P("ctx", "dp", "tp"), P(("dp", "ctx"), "tp")),
        check_vma=False,
    )
```

```python
import functools

import jax
import jax.numpy as jnp
from jax import lax
from jax.experimental import pallas as pl
from jax.experimental.pallas import tpu as pltpu
from jax.sharding import PartitionSpec as P

MESH = pl.DeviceIdType.MESH
BF16 = jnp.bfloat16
F32 = jnp.float32
HI = 2
CORES = 2
ROWS = 16
LANES = 128
PARTS = 4


def xor(a, bits):
    for bit in (1, 2, 4, 8):
        if bits & bit:
            a = a + bit - 2 * bit * ((a // bit) % 2)
    return a


def nt(a, b):
    return lax.dot_general(a, b, (((1,), (1,)), ((), ())), preferred_element_type=F32)


def tn(a, b):
    return lax.dot_general(a, b, (((0,), (0,)), ((), ())), preferred_element_type=F32)


def nn(a, b):
    return jnp.dot(a, b, preferred_element_type=F32)


def kernel(
    dims,
    tokens_hbm, ids_hbm, w_hbm, cot_hbm,
    hidden_hbm, wgrad_hbm, tgrad_hbm,
    hidden, wgrad, tgrad, tokens, ids, cot, place, rt, w, ysend, yrecv, g, r, acc, s, psend, precv, qsend, t, hsend, hrecv, wsend, wkeep, wrecv,
    in_sems, out_sems, y_ss, y_rs, gd_ss, gd_rs, gf_ss, gf_rs, r_ss, rf_ss, r_rs, s_ss, s_rs,
    p_ss, p_rs, t_ss, t_rs, h_ss, h_rs, x_ss, x_rs,
):
    n_z, n_ctx, n_lo, capacity = dims
    feat = tokens.shape[1]
    slots = cot.shape[0]
    cols = cot.shape[1] // PARTS
    half = feat // HI
    dp, e, j = lax.axis_index("dp"), lax.axis_index("ctx"), lax.axis_index("tp")
    z, hi = dp // HI, dp % HI
    lo, core = j // CORES, j % CORES
    waits = []

    def copy(src, dst, ssem, rsem, to):
        return pltpu.make_async_remote_copy(
            src_ref=src, dst_ref=dst, send_sem=ssem, recv_sem=rsem,
            device_id=to, device_id_type=MESH,
        )

    def send(*args):
        made = copy(*args)
        made.start()
        waits.append(made)

    stores = []

    def store(src, dst):
        made = pltpu.make_async_copy(src, dst, out_sems.at[len(stores)])
        made.start()
        stores.append(made)

    def on_y(d):
        return (dp, (e + d) % n_ctx, j)

    def on_z(k):
        return (k * HI + hi, e, j)

    def on_lo(o):
        return (dp, e, xor(lo, o) * CORES + core)

    other = (dp, e, lo * CORES + 1 - core)
    across = (z * HI + 1 - hi, e, j)

    loads = [
        pltpu.make_async_copy(src, dst, in_sems.at[i])
        for i, (src, dst) in enumerate(((ids_hbm, ids), (tokens_hbm, tokens), (cot_hbm, cot), (w_hbm, w)))
    ]
    for load in loads:
        load.start()

    partners = [on_y(d) for d in range(1, n_ctx)]
    partners += [on_z((z + d) % n_z) for d in range(1, n_z)]
    partners += [on_lo(o) for o in range(1, n_lo)]
    partners += [other, across]
    barrier = pltpu.get_barrier_semaphore()
    for to in partners:
        pl.semaphore_signal(barrier, inc=1, device_id=to, device_id_type=MESH)

    count, folds = tokens.shape[0], feat // LANES
    beyond = (capacity - ROWS) * folds
    loads[0].wait()
    name = lax.broadcasted_iota(jnp.int32, (n_ctx, count), 0)
    named = ((ids[0:1, :] == name) | (ids[1:2, :] == name)).astype(F32)
    earlier = lax.broadcasted_iota(jnp.int32, (count, count), 0) < lax.broadcasted_iota(jnp.int32, (count, count), 1)
    rank = jnp.where(named > 0.0, nn(named.astype(BF16), earlier.astype(F32).astype(BF16)), -1.0)

    def slot_of(row, kind):
        if kind == 0:
            return row
        slot = jnp.full_like(row, -2)
        for r in range(kind - 1, beyond, folds):
            slot = jnp.where(row == r, ROWS + r // folds, slot)
        return slot

    row = lax.broadcasted_iota(jnp.int32, (ROWS, count), 0)
    for kind in range(folds + 1):
        slot = slot_of(row, kind).astype(F32)
        for x in range(n_ctx):
            place[kind, x * ROWS:(x + 1) * ROWS, :] = (rank[x:x + 1, :] == slot).astype(F32).astype(BF16)

    def fold(mats, rows):
        wide = nn(mats[0], rows)
        tail = nn(mats[1], rows[:, 0:LANES])
        for f in range(1, folds):
            tail = tail + nn(mats[f + 1], rows[:, f * LANES:(f + 1) * LANES])
        return jnp.concatenate([wide, tail], axis=1).astype(BF16).reshape(ysend.shape)

    def unfold(mats, blocks, dot):
        wide = dot(mats[0], blocks[:, 0:feat])
        tail = blocks[:, feat:]
        return wide + jnp.concatenate([dot(mats[f + 1], tail) for f in range(folds)], axis=1)

    loads[1].wait()
    ysend[...] = fold(place, tokens[...])
    pl.semaphore_wait(barrier, len(partners))

    def spread(kind, rows_at):
        shape = [slots, n_ctx * ROWS] if rows_at == 0 else [n_ctx * ROWS, slots]
        want, col = lax.broadcasted_iota(jnp.int32, shape, rows_at), lax.broadcasted_iota(jnp.int32, shape, 1 - rows_at)
        within = slot_of(col & (ROWS - 1), kind)
        same = ((col >> (ROWS.bit_length() - 1)) * capacity + within == want) & (within >= 0)
        return same.astype(F32).astype(BF16)

    far = sorted(range(1, n_ctx), key=lambda d: -min(d, n_ctx - d))
    for d in far:
        send(ysend.at[(e + d) % n_ctx], yrecv.at[e], y_ss.at[d - 1], y_rs.at[d - 1], on_y(d))
    yrecv[e] = ysend[e]
    pack = [spread(kind, 0) for kind in range(folds + 1)]
    for d in far:
        copy(ysend.at[0], yrecv.at[(e - d + n_ctx) % n_ctx], y_ss.at[d - 1], y_rs.at[d - 1], on_y(d)).wait_recv()
    g[j] = unfold(pack, yrecv[...].reshape(-1, feat + LANES), nn).astype(BF16)

    near = [o for o in (2, 1) if o < n_lo]
    inner = (lo + 1) // 2 % 2 == 1
    end = 3
    direct = copy(g.at[j], g.at[j], gd_ss.at[n_lo - 1], gd_rs.at[n_lo - 1], on_lo(n_lo - 1))
    passed = xor(lo, n_lo // 2) * CORES + core
    through = copy(g.at[passed], g.at[passed], gd_ss.at[0], gd_rs.at[n_lo - 1], on_lo(1))
    send(g.at[j], g.at[j], gd_ss.at[near[0]], gd_rs.at[near[0]], on_lo(near[0]))
    if n_lo > end:

        @pl.when(inner)
        def _():
            direct.start()

    send(g.at[j], g.at[j], gf_ss.at[0], gf_rs.at[0], other)
    for o in near[1:]:
        send(g.at[j], g.at[j], gd_ss.at[o], gd_rs.at[o], on_lo(o))

    row_sender = (core + z + lo) % 2 == 0
    row_taker = core == z % CORES

    def rows_copy(o):
        k = xor(lo, o) * CORES + core
        return k, copy(g.at[k], r.at[z], r_ss.at[o], r_rs.at[z], on_z(k))

    def rows_start(o):
        k, made = rows_copy(o)

        @pl.when((k != z) & row_sender)
        def _():
            made.start()

    def project(k, first=False):
        @pl.loop(0, PARTS)
        def _(q):
            at = pl.ds(pl.multiple_of(q * cols, cols), cols)
            term = nn(g[k], w[pl.ds(pl.multiple_of(k * feat, feat), feat), at])
            acc[q] = term if first else acc[q] + term

    rows_start(0)
    loads[3].wait()
    project(j, True)
    k = lo * CORES + 1 - core
    copy(g.at[j], g.at[k], gf_ss.at[0], gf_rs.at[0], other).wait_recv()
    project(k)
    order = near + [end] * (n_lo > end)
    for o in order:
        k = xor(lo, o) * CORES + core
        copy(g.at[j], g.at[k], gd_ss.at[o], gd_rs.at[o], on_lo(o)).wait_recv()
        if n_lo > end and o == near[0]:

            @pl.when(inner)
            def _():
                through.start()

        send(g.at[k], g.at[k], gf_ss.at[o], gf_rs.at[o], other)
        rows_start(o)
        project(k)
    for o in order:
        k = xor(lo, o) * CORES + 1 - core
        copy(g.at[j], g.at[k], gf_ss.at[o], gf_rs.at[o], other).wait_recv()
        if o != order[-1]:
            project(k)
    last = k

    def reach(way, q):
        return n_z // 2 if q % 2 == way else n_z - 1 - n_z // 2

    def step_to(way):
        return on_z((z + 1) % n_z if way == 0 else (z + n_z - 1) % n_z)

    def own(q):
        for way in (0, 1):
            send(s.at[q, z], s.at[q, z], s_ss.at[way, q, 0], s_rs.at[way, q, 0], step_to(way))

    def step(q, d):
        for way in (0, 1):
            if d <= reach(way, q):
                src = (z - d + n_z) % n_z if way == 0 else (z + d) % n_z
                copy(s.at[q, z], s.at[q, src], s_ss.at[way, q, d - 1], s_rs.at[way, q, d - 1], step_to(way)).wait_recv()
                if d < reach(way, q):
                    send(s.at[q, src], s.at[q, src], s_ss.at[way, q, d], s_rs.at[way, q, d], step_to(way))

    loads[2].wait()
    for q in range(PARTS):
        at = slice(q * cols, (q + 1) * cols)
        p = acc[q] + nn(g[last], w[pl.ds(pl.multiple_of(last * feat, feat), feat), at])
        acc[q] = p
        gate = jax.nn.sigmoid(p)
        s[q, z] = (cot[:, at].astype(F32) * gate * (1.0 + p * (1.0 - gate))).astype(BF16)
        own(q)

    def back(k):
        rows = pl.ds(pl.multiple_of(k * feat, feat), feat)
        total = nt(s[0, z], w[rows, 0:cols])
        for q in range(1, PARTS):
            total = total + nt(s[q, z], w[rows, q * cols:(q + 1) * cols])
        return total

    for m in range(n_lo):
        psend[m] = back(m * CORES + 1 - core).astype(BF16)
        send(psend.at[m], precv.at[m], p_ss.at[m], p_rs.at[m], other)

    first, second = (0, 1), (2, 3)
    n_d = n_z // 2

    def steps(part, d):
        for q in part:
            step(q, d)

    r[z] = g[z]

    def rows_in(d):
        src = (z + d) % n_z
        copy(g.at[0], r.at[src], r_ss.at[0], r_rs.at[src], other).wait_recv()

    def rows_on(d):
        src = (z + d) % n_z
        return (
            copy(r.at[src], r.at[src], rf_ss.at[0, d - 1], r_rs.at[src], other),
            copy(r.at[src], r.at[src], rf_ss.at[1, d - 1], r_rs.at[src], on_lo(1)),
        )

    for d in range(1, n_z):

        @pl.when(row_taker & (lo % 2 == d % 2))
        def _():
            rows_in(d)
            for made in rows_on(d):
                made.start()

    steps(first, 1)

    for m in range(n_lo):
        copy(psend.at[m], precv.at[m], p_ss.at[m], p_rs.at[m], other).wait_recv()
    for o in (*range(1, n_lo), 0):
        m = xor(lo, o)
        qsend[o] = (back(m * CORES + core) + precv[m].astype(F32)).astype(BF16)
        if o:
            send(qsend.at[o], t.at[o], t_ss.at[o], t_rs.at[o], on_lo(o))

    if n_d > 2:
        steps(first, 2)
    steps(second, 1)

    for d in range(1, n_z):

        @pl.when(row_taker & (lo % 2 != d % 2))
        def _():
            rows_in(d)
            rows_on(d)[0].start()

        @pl.when(jnp.logical_not(row_taker))
        def _():
            rows_in(d)

    for d in range(3, n_d):
        steps(first, d)
        steps(second, d - 1)

    rt[...] = r[...].reshape(-1, feat).T
    for q in range(PARTS):
        p = acc[q]
        hidden[:, q * cols:(q + 1) * cols] = (p * jax.nn.sigmoid(p)).astype(BF16)
    store(hidden, hidden_hbm)

    def product(q, side):
        return nn(rt[pl.ds(pl.multiple_of(side * half, half), half), :], s[q].reshape(-1, cols))

    def theirs(q):
        wsend[q] = product(q, 1 - hi).astype(BF16)
        send(wsend.at[q], wrecv.at[q], x_ss.at[q], x_rs.at[q], across)

    steps(first, n_d)
    for q in first:
        theirs(q)
    if n_d > 2:
        steps(second, n_d - 1)

    summed = qsend[0].astype(F32)
    for o in range(1, n_lo):
        copy(qsend.at[o], t.at[o], t_ss.at[o], t_rs.at[o], on_lo(o)).wait_recv()
        summed = summed + t[o].astype(F32)
    hsend[...] = fold([spread(kind, 1) for kind in range(folds + 1)], summed.astype(BF16))
    for d in far:
        send(hsend.at[(e + d) % n_ctx], hrecv.at[e], h_ss.at[d - 1], h_rs.at[d - 1], on_y(d))
    hrecv[e] = hsend[e]

    for q in first:
        wkeep[q] = product(q, hi)
    steps(second, n_d)
    for q in second:
        theirs(q)
    for q in second:
        wkeep[q] = product(q, hi)

    for d in far:
        copy(hsend.at[0], hrecv.at[(e - d + n_ctx) % n_ctx], h_ss.at[d - 1], h_rs.at[d - 1], on_y(d)).wait_recv()
    tgrad[...] = unfold(place, hrecv[...].reshape(-1, feat + LANES), tn).astype(BF16)
    store(tgrad, tgrad_hbm)

    for q in range(PARTS):
        copy(wsend.at[q], wrecv.at[q], x_ss.at[q], x_rs.at[q], across).wait_recv()
        at = slice(q * cols, (q + 1) * cols)
        wgrad[:, at] = (wkeep[q] + wrecv[q].astype(F32)).astype(BF16)
        store(wgrad.at[:, at], wgrad_hbm.at[:, at])

    for made in waits:
        made.wait_send()
    for made in stores:
        made.wait()
    if n_lo > end:

        @pl.when(inner)
        def _():
            direct.wait_send()
            through.wait_send()
    for o in range(n_lo):
        k, made = rows_copy(o)

        @pl.when((k != z) & row_sender)
        def _():
            made.wait_send()

    for d in range(1, n_z):

        @pl.when(row_taker)
        def _():
            rows_on(d)[0].wait_send()

        @pl.when(row_taker & (lo % 2 == d % 2))
        def _():
            rows_on(d)[1].wait_send()


def per_device(tokens, expert_ids, weights, cotangent):
    n_ctx, n_tp, n_dp = lax.axis_size("ctx"), lax.axis_size("tp"), lax.axis_size("dp")
    n_z, n_lo = n_dp // HI, n_tp // CORES
    count, feat = tokens.shape
    slots, ff = cotangent.shape[2:]
    capacity = slots // n_ctx
    cols, half = ff // PARTS, feat // HI

    dma = pltpu.SemaphoreType.DMA
    hidden, wgrad, tgrad = pl.pallas_call(
        functools.partial(kernel, (n_z, n_ctx, n_lo, capacity)),
        out_shape=(
            jax.ShapeDtypeStruct((slots, ff), BF16),
            jax.ShapeDtypeStruct((half, ff), BF16),
            jax.ShapeDtypeStruct((count, feat), BF16),
        ),
        in_specs=[pl.BlockSpec(memory_space=pl.ANY)] * 4,
        out_specs=[pl.BlockSpec(memory_space=pl.ANY)] * 3,
        scratch_shapes=[
            pltpu.VMEM((slots, ff), BF16),
            pltpu.VMEM((half, ff), BF16),
            pltpu.VMEM((count, feat), BF16),
            pltpu.VMEM((count, feat), BF16),
            pltpu.VMEM((2, count), jnp.int32),
            pltpu.VMEM((slots, ff), BF16),
            pltpu.VMEM((feat // LANES + 1, n_ctx * ROWS, count), BF16),
            pltpu.VMEM((feat, n_z * slots), BF16),
            pltpu.VMEM(weights.shape[1:], BF16),
            pltpu.VMEM((n_ctx, ROWS, feat + LANES), BF16),
            pltpu.VMEM((n_ctx, ROWS, feat + LANES), BF16),
            pltpu.VMEM((n_tp, slots, feat), BF16),
            pltpu.VMEM((n_z, slots, feat), BF16),
            pltpu.VMEM((PARTS, slots, cols), F32),
            pltpu.VMEM((PARTS, n_z, slots, cols), BF16),
            pltpu.VMEM((n_lo, slots, feat), BF16),
            pltpu.VMEM((n_lo, slots, feat), BF16),
            pltpu.VMEM((n_lo, slots, feat), BF16),
            pltpu.VMEM((n_lo, slots, feat), BF16),
            pltpu.VMEM((n_ctx, ROWS, feat + LANES), BF16),
            pltpu.VMEM((n_ctx, ROWS, feat + LANES), BF16),
            pltpu.VMEM((PARTS, half, cols), BF16),
            pltpu.VMEM((PARTS, half, cols), F32),
            pltpu.VMEM((PARTS, half, cols), BF16),
            dma((4,)), dma((2 + PARTS,)),
            dma((n_ctx - 1,)), dma((n_ctx - 1,)),
            dma((n_lo,)), dma((n_lo,)),
            dma((n_lo,)), dma((n_lo,)),
            dma((n_lo,)), dma((2, n_z - 1)), dma((n_z,)),
            dma((2, PARTS, n_z // 2)), dma((2, PARTS, n_z // 2)),
            dma((n_lo,)), dma((n_lo,)),
            dma((n_lo,)), dma((n_lo,)),
            dma((n_ctx - 1,)), dma((n_ctx - 1,)),
            dma((PARTS,)), dma((PARTS,)),
        ],
        compiler_params=pltpu.CompilerParams(
            collective_id=0, has_side_effects=True, vmem_limit_bytes=48 * 1024 * 1024
        ),
    )(tokens, expert_ids.T, weights[0], cotangent[0, 0])
    return hidden[None, None], wgrad[None], tgrad


def solution(mesh):
    placed = (
        P(("dp", "ctx"), "tp"),
        P(("dp", "ctx"), None),
        P("ctx", None, "tp"),
        P("dp", "ctx", None, "tp"),
    )
    return jax.shard_map(
        per_device,
        mesh=mesh,
        in_specs=placed,
        out_specs=(P("dp", "ctx", None, "tp"), P("ctx", "dp", "tp"), P(("dp", "ctx"), "tp")),
        check_vma=False,
    )
```

```python
import functools

import jax
import jax.numpy as jnp
from jax import lax
from jax.experimental import pallas as pl
from jax.experimental.pallas import tpu as pltpu
from jax.sharding import PartitionSpec as P

MESH = pl.DeviceIdType.MESH
BF16 = jnp.bfloat16
F32 = jnp.float32
HI = 2
CORES = 2
ROWS = 16
LANES = 128
PARTS = 4


def xor(a, bits):
    for bit in (1, 2, 4, 8):
        if bits & bit:
            a = a + bit - 2 * bit * ((a // bit) % 2)
    return a


def nt(a, b):
    return lax.dot_general(a, b, (((1,), (1,)), ((), ())), preferred_element_type=F32)


def tn(a, b):
    return lax.dot_general(a, b, (((0,), (0,)), ((), ())), preferred_element_type=F32)


def nn(a, b):
    return jnp.dot(a, b, preferred_element_type=F32)


def kernel(
    dims,
    small, w_hbm,
    wide_out,
    hidden, wgrad, tgrad, tokens, ids, cot, place, rt, w, ysend, yrecv, g, r, acc, s, psend, precv, qsend, t, hsend, hrecv, wsend, wkeep, wrecv,
    in_sems, out_sems, y_ss, y_rs, gd_ss, gd_rs, gf_ss, gf_rs, r_ss, rf_ss, r_rs, s_ss, s_rs,
    p_ss, p_rs, t_ss, t_rs, h_ss, h_rs, x_ss, x_rs,
):
    n_z, n_ctx, n_lo, capacity = dims
    slots, count, feat = cot.shape[0], tokens.shape[0], tokens.shape[1]
    cot_hbm, tokens_hbm = small.at[0:slots], small.at[slots:slots + count, 0:feat]
    ids_hbm = small.at[slots + count:, 0:ids.shape[1]]
    half = feat // HI
    hidden_hbm, wgrad_hbm = wide_out.at[0:slots], wide_out.at[slots:slots + half]
    tgrad_hbm = wide_out.at[slots + half:, 0:feat]
    cols = cot.shape[1] // PARTS
    dp, e, j = lax.axis_index("dp"), lax.axis_index("ctx"), lax.axis_index("tp")
    z, hi = dp // HI, dp % HI
    lo, core = j // CORES, j % CORES
    waits = []

    def copy(src, dst, ssem, rsem, to):
        return pltpu.make_async_remote_copy(
            src_ref=src, dst_ref=dst, send_sem=ssem, recv_sem=rsem,
            device_id=to, device_id_type=MESH,
        )

    def send(*args):
        made = copy(*args)
        made.start()
        waits.append(made)

    stores = []

    def store(src, dst):
        made = pltpu.make_async_copy(src, dst, out_sems.at[len(stores)])
        made.start()
        stores.append(made)

    def on_y(d):
        return (dp, (e + d) % n_ctx, j)

    def on_z(k):
        return (k * HI + hi, e, j)

    def on_lo(o):
        return (dp, e, xor(lo, o) * CORES + core)

    other = (dp, e, lo * CORES + 1 - core)
    across = (z * HI + 1 - hi, e, j)

    loads = [
        pltpu.make_async_copy(src, dst, in_sems.at[i])
        for i, (src, dst) in enumerate(((ids_hbm, ids), (tokens_hbm, tokens), (cot_hbm, cot), (w_hbm, w)))
    ]
    for load in loads:
        load.start()

    partners = [on_y(d) for d in range(1, n_ctx)]
    partners += [on_z((z + d) % n_z) for d in range(1, n_z)]
    partners += [on_lo(o) for o in range(1, n_lo)]
    partners += [other, across]
    barrier = pltpu.get_barrier_semaphore()
    for to in partners:
        pl.semaphore_signal(barrier, inc=1, device_id=to, device_id_type=MESH)

    folds = feat // LANES
    beyond = (capacity - ROWS) * folds
    loads[0].wait()
    name = lax.broadcasted_iota(jnp.int32, (n_ctx, count), 0).astype(F32)
    named = ((ids[0:1, 0:count].astype(F32) == name) | (ids[1:2, 0:count].astype(F32) == name)).astype(F32)
    earlier = lax.broadcasted_iota(jnp.int32, (count, count), 0) < lax.broadcasted_iota(jnp.int32, (count, count), 1)
    rank = jnp.where(named > 0.0, nn(named.astype(BF16), earlier.astype(F32).astype(BF16)), -1.0)

    def slot_of(row, kind):
        if kind == 0:
            return row
        slot = jnp.full_like(row, -2)
        for r in range(kind - 1, beyond, folds):
            slot = jnp.where(row == r, ROWS + r // folds, slot)
        return slot

    row = lax.broadcasted_iota(jnp.int32, (ROWS, count), 0)
    for kind in range(folds + 1):
        slot = slot_of(row, kind).astype(F32)
        for x in range(n_ctx):
            place[kind, x * ROWS:(x + 1) * ROWS, :] = (rank[x:x + 1, :] == slot).astype(F32).astype(BF16)

    def fold(mats, rows):
        wide = nn(mats[0], rows)
        tail = nn(mats[1], rows[:, 0:LANES])
        for f in range(1, folds):
            tail = tail + nn(mats[f + 1], rows[:, f * LANES:(f + 1) * LANES])
        return jnp.concatenate([wide, tail], axis=1).astype(BF16).reshape(ysend.shape)

    def unfold(mats, blocks, dot):
        wide = dot(mats[0], blocks[:, 0:feat])
        tail = blocks[:, feat:]
        return wide + jnp.concatenate([dot(mats[f + 1], tail) for f in range(folds)], axis=1)

    loads[1].wait()
    ysend[...] = fold(place, tokens[...])
    pl.semaphore_wait(barrier, len(partners))

    def spread(kind, rows_at):
        shape = [slots, n_ctx * ROWS] if rows_at == 0 else [n_ctx * ROWS, slots]
        want, col = lax.broadcasted_iota(jnp.int32, shape, rows_at), lax.broadcasted_iota(jnp.int32, shape, 1 - rows_at)
        within = slot_of(col & (ROWS - 1), kind)
        same = ((col >> (ROWS.bit_length() - 1)) * capacity + within == want) & (within >= 0)
        return same.astype(F32).astype(BF16)

    far = sorted(range(1, n_ctx), key=lambda d: -min(d, n_ctx - d))
    for d in far:
        send(ysend.at[(e + d) % n_ctx], yrecv.at[e], y_ss.at[d - 1], y_rs.at[d - 1], on_y(d))
    yrecv[e] = ysend[e]
    pack = [spread(kind, 0) for kind in range(folds + 1)]
    for d in far:
        copy(ysend.at[0], yrecv.at[(e - d + n_ctx) % n_ctx], y_ss.at[d - 1], y_rs.at[d - 1], on_y(d)).wait_recv()
    g[j] = unfold(pack, yrecv[...].reshape(-1, feat + LANES), nn).astype(BF16)

    near = [o for o in (2, 1) if o < n_lo]
    inner = (lo + 1) // 2 % 2 == 1
    end = 3
    direct = copy(g.at[j], g.at[j], gd_ss.at[n_lo - 1], gd_rs.at[n_lo - 1], on_lo(n_lo - 1))
    passed = xor(lo, n_lo // 2) * CORES + core
    through = copy(g.at[passed], g.at[passed], gd_ss.at[0], gd_rs.at[n_lo - 1], on_lo(1))
    send(g.at[j], g.at[j], gd_ss.at[near[0]], gd_rs.at[near[0]], on_lo(near[0]))
    if n_lo > end:

        @pl.when(inner)
        def _():
            direct.start()

    send(g.at[j], g.at[j], gf_ss.at[0], gf_rs.at[0], other)
    for o in near[1:]:
        send(g.at[j], g.at[j], gd_ss.at[o], gd_rs.at[o], on_lo(o))

    row_sender = (core + z + lo) % 2 == 0
    row_taker = core == z % CORES

    def rows_copy(o):
        k = xor(lo, o) * CORES + core
        return k, copy(g.at[k], r.at[z], r_ss.at[o], r_rs.at[z], on_z(k))

    def rows_start(o):
        k, made = rows_copy(o)

        @pl.when((k != z) & row_sender)
        def _():
            made.start()

    def project(k, first=False):
        @pl.loop(0, PARTS)
        def _(q):
            at = pl.ds(pl.multiple_of(q * cols, cols), cols)
            term = nn(g[k], w[pl.ds(pl.multiple_of(k * feat, feat), feat), at])
            acc[q] = term if first else acc[q] + term

    rows_start(0)
    loads[3].wait()
    project(j, True)
    k = lo * CORES + 1 - core
    copy(g.at[j], g.at[k], gf_ss.at[0], gf_rs.at[0], other).wait_recv()
    project(k)
    order = near + [end] * (n_lo > end)
    for o in order:
        k = xor(lo, o) * CORES + core
        copy(g.at[j], g.at[k], gd_ss.at[o], gd_rs.at[o], on_lo(o)).wait_recv()
        if n_lo > end and o == near[0]:

            @pl.when(inner)
            def _():
                through.start()

        send(g.at[k], g.at[k], gf_ss.at[o], gf_rs.at[o], other)
        rows_start(o)
        project(k)
    for o in order:
        k = xor(lo, o) * CORES + 1 - core
        copy(g.at[j], g.at[k], gf_ss.at[o], gf_rs.at[o], other).wait_recv()
        if o != order[-1]:
            project(k)
    last = k

    def reach(way, q):
        return n_z // 2 if q % 2 == way else n_z - 1 - n_z // 2

    def step_to(way):
        return on_z((z + 1) % n_z if way == 0 else (z + n_z - 1) % n_z)

    def own(q):
        for way in (0, 1):
            send(s.at[q, z], s.at[q, z], s_ss.at[way, q, 0], s_rs.at[way, q, 0], step_to(way))

    def step(q, d):
        for way in (0, 1):
            if d <= reach(way, q):
                src = (z - d + n_z) % n_z if way == 0 else (z + d) % n_z
                copy(s.at[q, z], s.at[q, src], s_ss.at[way, q, d - 1], s_rs.at[way, q, d - 1], step_to(way)).wait_recv()
                if d < reach(way, q):
                    send(s.at[q, src], s.at[q, src], s_ss.at[way, q, d], s_rs.at[way, q, d], step_to(way))

    loads[2].wait()
    for q in range(PARTS):
        at = slice(q * cols, (q + 1) * cols)
        p = acc[q] + nn(g[last], w[pl.ds(pl.multiple_of(last * feat, feat), feat), at])
        acc[q] = p
        gate = jax.nn.sigmoid(p)
        s[q, z] = (cot[:, at].astype(F32) * gate * (1.0 + p * (1.0 - gate))).astype(BF16)
        own(q)

    def back(k):
        rows = pl.ds(pl.multiple_of(k * feat, feat), feat)
        total = nt(s[0, z], w[rows, 0:cols])
        for q in range(1, PARTS):
            total = total + nt(s[q, z], w[rows, q * cols:(q + 1) * cols])
        return total

    for m in range(n_lo):
        psend[m] = back(m * CORES + 1 - core).astype(BF16)
        send(psend.at[m], precv.at[m], p_ss.at[m], p_rs.at[m], other)

    first, second = (0, 1), (2, 3)
    n_d = n_z // 2

    def steps(part, d):
        for q in part:
            step(q, d)

    r[z] = g[z]

    def rows_in(d):
        src = (z + d) % n_z
        copy(g.at[0], r.at[src], r_ss.at[0], r_rs.at[src], other).wait_recv()

    def rows_on(d):
        src = (z + d) % n_z
        return (
            copy(r.at[src], r.at[src], rf_ss.at[0, d - 1], r_rs.at[src], other),
            copy(r.at[src], r.at[src], rf_ss.at[1, d - 1], r_rs.at[src], on_lo(1)),
        )

    for d in range(1, n_z):

        @pl.when(row_taker & (lo % 2 == d % 2))
        def _():
            rows_in(d)
            for made in rows_on(d):
                made.start()

    steps(first, 1)

    for m in range(n_lo):
        copy(psend.at[m], precv.at[m], p_ss.at[m], p_rs.at[m], other).wait_recv()
    for o in (*range(1, n_lo), 0):
        m = xor(lo, o)
        qsend[o] = (back(m * CORES + core) + precv[m].astype(F32)).astype(BF16)
        if o:
            send(qsend.at[o], t.at[o], t_ss.at[o], t_rs.at[o], on_lo(o))

    if n_d > 2:
        steps(first, 2)
    steps(second, 1)

    for d in range(1, n_z):

        @pl.when(row_taker & (lo % 2 != d % 2))
        def _():
            rows_in(d)
            rows_on(d)[0].start()

        @pl.when(jnp.logical_not(row_taker))
        def _():
            rows_in(d)

    for d in range(3, n_d):
        steps(first, d)
        steps(second, d - 1)

    rt[...] = r[...].reshape(-1, feat).T
    for q in range(PARTS):
        p = acc[q]
        hidden[:, q * cols:(q + 1) * cols] = (p * jax.nn.sigmoid(p)).astype(BF16)
    store(hidden, hidden_hbm)

    def product(q, side):
        return nn(rt[pl.ds(pl.multiple_of(side * half, half), half), :], s[q].reshape(-1, cols))

    def theirs(q):
        wsend[q] = product(q, 1 - hi).astype(BF16)
        send(wsend.at[q], wrecv.at[q], x_ss.at[q], x_rs.at[q], across)

    for q in first:
        step(q, n_d)
        theirs(q)
    if n_d > 2:
        steps(second, n_d - 1)

    summed = qsend[0].astype(F32)
    for o in range(1, n_lo):
        copy(qsend.at[o], t.at[o], t_ss.at[o], t_rs.at[o], on_lo(o)).wait_recv()
        summed = summed + t[o].astype(F32)
    hsend[...] = fold([spread(kind, 1) for kind in range(folds + 1)], summed.astype(BF16))
    for d in far:
        send(hsend.at[(e + d) % n_ctx], hrecv.at[e], h_ss.at[d - 1], h_rs.at[d - 1], on_y(d))
    hrecv[e] = hsend[e]

    for q in first:
        wkeep[q] = product(q, hi)
    for q in second:
        step(q, n_d)
        theirs(q)
    for q in second:
        wkeep[q] = product(q, hi)

    for d in far:
        copy(hsend.at[0], hrecv.at[(e - d + n_ctx) % n_ctx], h_ss.at[d - 1], h_rs.at[d - 1], on_y(d)).wait_recv()
    tgrad[...] = unfold(place, hrecv[...].reshape(-1, feat + LANES), tn).astype(BF16)
    store(tgrad, tgrad_hbm)

    for q in range(PARTS):
        copy(wsend.at[q], wrecv.at[q], x_ss.at[q], x_rs.at[q], across).wait_recv()
        at = slice(q * cols, (q + 1) * cols)
        wgrad[:, at] = (wkeep[q] + wrecv[q].astype(F32)).astype(BF16)
        store(wgrad.at[:, at], wgrad_hbm.at[:, at])

    for made in waits:
        made.wait_send()
    for made in stores:
        made.wait()
    if n_lo > end:

        @pl.when(inner)
        def _():
            direct.wait_send()
            through.wait_send()
    for o in range(n_lo):
        k, made = rows_copy(o)

        @pl.when((k != z) & row_sender)
        def _():
            made.wait_send()

    for d in range(1, n_z):

        @pl.when(row_taker)
        def _():
            rows_on(d)[0].wait_send()

        @pl.when(row_taker & (lo % 2 == d % 2))
        def _():
            rows_on(d)[1].wait_send()


def per_device(tokens, expert_ids, weights, cotangent):
    n_ctx, n_tp, n_dp = lax.axis_size("ctx"), lax.axis_size("tp"), lax.axis_size("dp")
    n_z, n_lo = n_dp // HI, n_tp // CORES
    count, feat = tokens.shape
    slots, ff = cotangent.shape[2:]
    capacity = slots // n_ctx
    cols, half = ff // PARTS, feat // HI

    dma = pltpu.SemaphoreType.DMA
    def wide(rows, height):
        return jnp.pad(rows, ((0, height - rows.shape[0]), (0, ff - rows.shape[1])))

    small = jnp.concatenate([cotangent[0, 0], wide(tokens, count), wide(expert_ids.T.astype(BF16), 16)])
    out = pl.pallas_call(
        functools.partial(kernel, (n_z, n_ctx, n_lo, capacity)),
        out_shape=jax.ShapeDtypeStruct((slots + half + count, ff), BF16),
        in_specs=[pl.BlockSpec(memory_space=pl.ANY)] * 2,
        out_specs=pl.BlockSpec(memory_space=pl.ANY),
        scratch_shapes=[
            pltpu.VMEM((slots, ff), BF16),
            pltpu.VMEM((half, ff), BF16),
            pltpu.VMEM((count, feat), BF16),
            pltpu.VMEM((count, feat), BF16),
            pltpu.VMEM((16, LANES), BF16),
            pltpu.VMEM((slots, ff), BF16),
            pltpu.VMEM((feat // LANES + 1, n_ctx * ROWS, count), BF16),
            pltpu.VMEM((feat, n_z * slots), BF16),
            pltpu.VMEM(weights.shape[1:], BF16),
            pltpu.VMEM((n_ctx, ROWS, feat + LANES), BF16),
            pltpu.VMEM((n_ctx, ROWS, feat + LANES), BF16),
            pltpu.VMEM((n_tp, slots, feat), BF16),
            pltpu.VMEM((n_z, slots, feat), BF16),
            pltpu.VMEM((PARTS, slots, cols), F32),
            pltpu.VMEM((PARTS, n_z, slots, cols), BF16),
            pltpu.VMEM((n_lo, slots, feat), BF16),
            pltpu.VMEM((n_lo, slots, feat), BF16),
            pltpu.VMEM((n_lo, slots, feat), BF16),
            pltpu.VMEM((n_lo, slots, feat), BF16),
            pltpu.VMEM((n_ctx, ROWS, feat + LANES), BF16),
            pltpu.VMEM((n_ctx, ROWS, feat + LANES), BF16),
            pltpu.VMEM((PARTS, half, cols), BF16),
            pltpu.VMEM((PARTS, half, cols), F32),
            pltpu.VMEM((PARTS, half, cols), BF16),
            dma((4,)), dma((2 + PARTS,)),
            dma((n_ctx - 1,)), dma((n_ctx - 1,)),
            dma((n_lo,)), dma((n_lo,)),
            dma((n_lo,)), dma((n_lo,)),
            dma((n_lo,)), dma((2, n_z - 1)), dma((n_z,)),
            dma((2, PARTS, n_z // 2)), dma((2, PARTS, n_z // 2)),
            dma((n_lo,)), dma((n_lo,)),
            dma((n_lo,)), dma((n_lo,)),
            dma((n_ctx - 1,)), dma((n_ctx - 1,)),
            dma((PARTS,)), dma((PARTS,)),
        ],
        compiler_params=pltpu.CompilerParams(
            collective_id=0, has_side_effects=True, vmem_limit_bytes=48 * 1024 * 1024
        ),
    )(small, weights[0])
    return out[None, None, :slots], out[None, slots:slots + half], out[slots + half:, :feat]


def solution(mesh):
    placed = (
        P(("dp", "ctx"), "tp"),
        P(("dp", "ctx"), None),
        P("ctx", None, "tp"),
        P("dp", "ctx", None, "tp"),
    )
    return jax.shard_map(
        per_device,
        mesh=mesh,
        in_specs=placed,
        out_specs=(P("dp", "ctx", None, "tp"), P("ctx", "dp", "tp"), P(("dp", "ctx"), "tp")),
        check_vma=False,
    )
```

```python
import functools

import jax
import jax.numpy as jnp
from jax import lax
from jax.experimental import pallas as pl
from jax.experimental.pallas import tpu as pltpu
from jax.sharding import PartitionSpec as P

MESH = pl.DeviceIdType.MESH
BF16 = jnp.bfloat16
F32 = jnp.float32
HI = 2
CORES = 2
ROWS = 16
LANES = 128
PARTS = 4


def xor(a, bits):
    for bit in (1, 2, 4, 8):
        if bits & bit:
            a = a + bit - 2 * bit * ((a // bit) % 2)
    return a


def nt(a, b):
    return lax.dot_general(a, b, (((1,), (1,)), ((), ())), preferred_element_type=F32)


def tn(a, b):
    return lax.dot_general(a, b, (((0,), (0,)), ((), ())), preferred_element_type=F32)


def nn(a, b):
    return jnp.dot(a, b, preferred_element_type=F32)


def kernel(
    dims,
    small, w_hbm,
    wide_out,
    hidden, wgrad, tgrad, tokens, ids, cot, place, rt, w, ysend, yrecv, g, r, acc, s, psend, precv, qsend, t, hsend, hrecv, wsend, wkeep, wrecv,
    in_sems, out_sems, y_ss, y_rs, gd_ss, gd_rs, gf_ss, gf_rs, r_ss, rf_ss, r_rs, s_ss, s_rs,
    p_ss, p_rs, t_ss, t_rs, h_ss, h_rs, x_ss, x_rs,
):
    n_z, n_ctx, n_lo, capacity = dims
    slots, count, feat = cot.shape[0], tokens.shape[0], tokens.shape[1]
    cot_hbm, tokens_hbm = small.at[0:slots], small.at[slots:slots + count, 0:feat]
    ids_hbm = small.at[slots + count:, 0:ids.shape[1]]
    half = feat // HI
    hidden_hbm, wgrad_hbm = wide_out.at[0:slots], wide_out.at[slots:slots + half]
    tgrad_hbm = wide_out.at[slots + half:, 0:feat]
    cols = cot.shape[1] // PARTS
    dp, e, j = lax.axis_index("dp"), lax.axis_index("ctx"), lax.axis_index("tp")
    z, hi = dp // HI, dp % HI
    lo, core = j // CORES, j % CORES
    waits = []

    def copy(src, dst, ssem, rsem, to):
        return pltpu.make_async_remote_copy(
            src_ref=src, dst_ref=dst, send_sem=ssem, recv_sem=rsem,
            device_id=to, device_id_type=MESH,
        )

    def send(*args):
        made = copy(*args)
        made.start()
        waits.append(made)

    stores = []

    def store(src, dst):
        made = pltpu.make_async_copy(src, dst, out_sems.at[len(stores)])
        made.start()
        stores.append(made)

    def on_y(d):
        return (dp, (e + d) % n_ctx, j)

    def on_z(k):
        return (k * HI + hi, e, j)

    def on_lo(o):
        return (dp, e, xor(lo, o) * CORES + core)

    other = (dp, e, lo * CORES + 1 - core)
    across = (z * HI + 1 - hi, e, j)

    loads = [
        pltpu.make_async_copy(src, dst, in_sems.at[i])
        for i, (src, dst) in enumerate(((ids_hbm, ids), (tokens_hbm, tokens), (cot_hbm, cot), (w_hbm, w)))
    ]
    for load in loads:
        load.start()

    partners = [on_y(d) for d in range(1, n_ctx)]
    partners += [on_z((z + d) % n_z) for d in range(1, n_z)]
    partners += [on_lo(o) for o in range(1, n_lo)]
    partners += [other, across]
    barrier = pltpu.get_barrier_semaphore()
    for to in partners:
        pl.semaphore_signal(barrier, inc=1, device_id=to, device_id_type=MESH)

    folds = feat // LANES
    beyond = (capacity - ROWS) * folds
    loads[0].wait()
    name = lax.broadcasted_iota(jnp.int32, (n_ctx, count), 0).astype(F32)
    named = ((ids[0:1, 0:count].astype(F32) == name) | (ids[1:2, 0:count].astype(F32) == name)).astype(F32)
    earlier = lax.broadcasted_iota(jnp.int32, (count, count), 0) < lax.broadcasted_iota(jnp.int32, (count, count), 1)
    rank = jnp.where(named > 0.0, nn(named.astype(BF16), earlier.astype(F32).astype(BF16)), -1.0)

    def slot_of(row, kind):
        if kind == 0:
            return row
        slot = jnp.full_like(row, -2)
        for r in range(kind - 1, beyond, folds):
            slot = jnp.where(row == r, ROWS + r // folds, slot)
        return slot

    row = lax.broadcasted_iota(jnp.int32, (ROWS, count), 0)
    for kind in range(folds + 1):
        slot = slot_of(row, kind).astype(F32)
        for x in range(n_ctx):
            place[kind, x * ROWS:(x + 1) * ROWS, :] = (rank[x:x + 1, :] == slot).astype(F32).astype(BF16)

    def fold(mats, rows):
        wide = nn(mats[0], rows)
        tail = nn(mats[1], rows[:, 0:LANES])
        for f in range(1, folds):
            tail = tail + nn(mats[f + 1], rows[:, f * LANES:(f + 1) * LANES])
        return jnp.concatenate([wide, tail], axis=1).astype(BF16).reshape(ysend.shape)

    def unfold(mats, blocks, dot):
        wide = dot(mats[0], blocks[:, 0:feat])
        tail = blocks[:, feat:]
        return wide + jnp.concatenate([dot(mats[f + 1], tail) for f in range(folds)], axis=1)

    loads[1].wait()
    ysend[...] = fold(place, tokens[...])
    pl.semaphore_wait(barrier, len(partners))

    def spread(kind, rows_at):
        shape = [slots, n_ctx * ROWS] if rows_at == 0 else [n_ctx * ROWS, slots]
        want, col = lax.broadcasted_iota(jnp.int32, shape, rows_at), lax.broadcasted_iota(jnp.int32, shape, 1 - rows_at)
        within = slot_of(col & (ROWS - 1), kind)
        same = ((col >> (ROWS.bit_length() - 1)) * capacity + within == want) & (within >= 0)
        return same.astype(F32).astype(BF16)

    far = sorted(range(1, n_ctx), key=lambda d: -min(d, n_ctx - d))
    for d in far:
        send(ysend.at[(e + d) % n_ctx], yrecv.at[e], y_ss.at[d - 1], y_rs.at[d - 1], on_y(d))
    yrecv[e] = ysend[e]
    pack = [spread(kind, 0) for kind in range(folds + 1)]
    for d in far:
        copy(ysend.at[0], yrecv.at[(e - d + n_ctx) % n_ctx], y_ss.at[d - 1], y_rs.at[d - 1], on_y(d)).wait_recv()
    g[j] = unfold(pack, yrecv[...].reshape(-1, feat + LANES), nn).astype(BF16)

    near = [o for o in (2, 1) if o < n_lo]
    inner = (lo + 1) // 2 % 2 == 1
    end = 3
    direct = copy(g.at[j], g.at[j], gd_ss.at[n_lo - 1], gd_rs.at[n_lo - 1], on_lo(n_lo - 1))
    passed = xor(lo, n_lo // 2) * CORES + core
    through = copy(g.at[passed], g.at[passed], gd_ss.at[0], gd_rs.at[n_lo - 1], on_lo(1))
    send(g.at[j], g.at[j], gd_ss.at[near[0]], gd_rs.at[near[0]], on_lo(near[0]))
    if n_lo > end:

        @pl.when(inner)
        def _():
            direct.start()

    send(g.at[j], g.at[j], gf_ss.at[0], gf_rs.at[0], other)
    for o in near[1:]:
        send(g.at[j], g.at[j], gd_ss.at[o], gd_rs.at[o], on_lo(o))

    row_sender = (core + z + lo) % 2 == 0
    row_taker = core == z % CORES

    def rows_copy(o):
        k = xor(lo, o) * CORES + core
        return k, copy(g.at[k], r.at[z], r_ss.at[o], r_rs.at[z], on_z(k))

    def rows_start(o):
        k, made = rows_copy(o)

        @pl.when((k != z) & row_sender)
        def _():
            made.start()

    def project(k, first=False):
        @pl.loop(0, PARTS)
        def _(q):
            at = pl.ds(pl.multiple_of(q * cols, cols), cols)
            term = nn(g[k], w[pl.ds(pl.multiple_of(k * feat, feat), feat), at])
            acc[q] = term if first else acc[q] + term

    rows_start(0)
    loads[3].wait()
    project(j, True)
    k = lo * CORES + 1 - core
    copy(g.at[j], g.at[k], gf_ss.at[0], gf_rs.at[0], other).wait_recv()
    project(k)
    order = near + [end] * (n_lo > end)
    for o in order:
        k = xor(lo, o) * CORES + core
        copy(g.at[j], g.at[k], gd_ss.at[o], gd_rs.at[o], on_lo(o)).wait_recv()
        if n_lo > end and o == near[0]:

            @pl.when(inner)
            def _():
                through.start()

        send(g.at[k], g.at[k], gf_ss.at[o], gf_rs.at[o], other)
        rows_start(o)
        project(k)
    for o in order:
        k = xor(lo, o) * CORES + 1 - core
        copy(g.at[j], g.at[k], gf_ss.at[o], gf_rs.at[o], other).wait_recv()
        if o != order[-1]:
            project(k)
    last = k

    def reach(way, q):
        return n_z // 2 if q % 2 == way else n_z - 1 - n_z // 2

    def step_to(way):
        return on_z((z + 1) % n_z if way == 0 else (z + n_z - 1) % n_z)

    def own(q):
        for way in (0, 1):
            send(s.at[q, z], s.at[q, z], s_ss.at[way, q, 0], s_rs.at[way, q, 0], step_to(way))

    def step(q, d):
        for way in (0, 1):
            if d <= reach(way, q):
                src = (z - d + n_z) % n_z if way == 0 else (z + d) % n_z
                copy(s.at[q, z], s.at[q, src], s_ss.at[way, q, d - 1], s_rs.at[way, q, d - 1], step_to(way)).wait_recv()
                if d < reach(way, q):
                    send(s.at[q, src], s.at[q, src], s_ss.at[way, q, d], s_rs.at[way, q, d], step_to(way))

    loads[2].wait()
    for q in range(PARTS):
        at = slice(q * cols, (q + 1) * cols)
        p = acc[q] + nn(g[last], w[pl.ds(pl.multiple_of(last * feat, feat), feat), at])
        acc[q] = p
        gate = jax.nn.sigmoid(p)
        s[q, z] = (cot[:, at].astype(F32) * gate * (1.0 + p * (1.0 - gate))).astype(BF16)
        if q < PARTS - 1:
            own(q)

    def back(k):
        rows = pl.ds(pl.multiple_of(k * feat, feat), feat)
        total = nt(s[0, z], w[rows, 0:cols])
        for q in range(1, PARTS):
            total = total + nt(s[q, z], w[rows, q * cols:(q + 1) * cols])
        return total

    for m in range(n_lo):
        psend[m] = back(m * CORES + 1 - core).astype(BF16)
        send(psend.at[m], precv.at[m], p_ss.at[m], p_rs.at[m], other)

    first, second = (0, 1), (2, 3)
    n_d = n_z // 2

    def steps(part, d):
        for q in part:
            step(q, d)

    r[z] = g[z]

    def rows_in(d):
        src = (z + d) % n_z
        copy(g.at[0], r.at[src], r_ss.at[0], r_rs.at[src], other).wait_recv()

    def rows_on(d):
        src = (z + d) % n_z
        return (
            copy(r.at[src], r.at[src], rf_ss.at[0, d - 1], r_rs.at[src], other),
            copy(r.at[src], r.at[src], rf_ss.at[1, d - 1], r_rs.at[src], on_lo(1)),
        )

    for d in range(1, n_z):

        @pl.when(row_taker & (lo % 2 == d % 2))
        def _():
            rows_in(d)
            for made in rows_on(d):
                made.start()

    steps(first, 1)
    own(PARTS - 1)

    for m in range(n_lo):
        copy(psend.at[m], precv.at[m], p_ss.at[m], p_rs.at[m], other).wait_recv()
    for o in (*range(1, n_lo), 0):
        m = xor(lo, o)
        qsend[o] = (back(m * CORES + core) + precv[m].astype(F32)).astype(BF16)
        if o:
            send(qsend.at[o], t.at[o], t_ss.at[o], t_rs.at[o], on_lo(o))

    if n_d > 2:
        steps(first, 2)
    steps(second, 1)

    for d in range(1, n_z):

        @pl.when(row_taker & (lo % 2 != d % 2))
        def _():
            rows_in(d)
            rows_on(d)[0].start()

        @pl.when(jnp.logical_not(row_taker))
        def _():
            rows_in(d)

    for d in range(3, n_d):
        steps(first, d)
        steps(second, d - 1)

    rt[...] = r[...].reshape(-1, feat).T
    for q in range(PARTS):
        p = acc[q]
        hidden[:, q * cols:(q + 1) * cols] = (p * jax.nn.sigmoid(p)).astype(BF16)
    store(hidden, hidden_hbm)

    def product(q, side):
        return nn(rt[pl.ds(pl.multiple_of(side * half, half), half), :], s[q].reshape(-1, cols))

    def theirs(q):
        wsend[q] = product(q, 1 - hi).astype(BF16)
        send(wsend.at[q], wrecv.at[q], x_ss.at[q], x_rs.at[q], across)

    for q in first:
        step(q, n_d)
        theirs(q)
    if n_d > 2:
        steps(second, n_d - 1)

    summed = qsend[0].astype(F32)
    for o in range(1, n_lo):
        copy(qsend.at[o], t.at[o], t_ss.at[o], t_rs.at[o], on_lo(o)).wait_recv()
        summed = summed + t[o].astype(F32)
    hsend[...] = fold([spread(kind, 1) for kind in range(folds + 1)], summed.astype(BF16))
    for d in far:
        send(hsend.at[(e + d) % n_ctx], hrecv.at[e], h_ss.at[d - 1], h_rs.at[d - 1], on_y(d))
    hrecv[e] = hsend[e]

    for q in first:
        wkeep[q] = product(q, hi)
    for q in second:
        step(q, n_d)
        theirs(q)
    for q in second:
        wkeep[q] = product(q, hi)

    for d in far:
        copy(hsend.at[0], hrecv.at[(e - d + n_ctx) % n_ctx], h_ss.at[d - 1], h_rs.at[d - 1], on_y(d)).wait_recv()
    tgrad[...] = unfold(place, hrecv[...].reshape(-1, feat + LANES), tn).astype(BF16)
    store(tgrad, tgrad_hbm)

    for q in range(PARTS):
        copy(wsend.at[q], wrecv.at[q], x_ss.at[q], x_rs.at[q], across).wait_recv()
        at = slice(q * cols, (q + 1) * cols)
        wgrad[:, at] = (wkeep[q] + wrecv[q].astype(F32)).astype(BF16)
        store(wgrad.at[:, at], wgrad_hbm.at[:, at])

    for made in waits:
        made.wait_send()
    for made in stores:
        made.wait()
    if n_lo > end:

        @pl.when(inner)
        def _():
            direct.wait_send()
            through.wait_send()
    for o in range(n_lo):
        k, made = rows_copy(o)

        @pl.when((k != z) & row_sender)
        def _():
            made.wait_send()

    for d in range(1, n_z):

        @pl.when(row_taker)
        def _():
            rows_on(d)[0].wait_send()

        @pl.when(row_taker & (lo % 2 == d % 2))
        def _():
            rows_on(d)[1].wait_send()


def per_device(tokens, expert_ids, weights, cotangent):
    n_ctx, n_tp, n_dp = lax.axis_size("ctx"), lax.axis_size("tp"), lax.axis_size("dp")
    n_z, n_lo = n_dp // HI, n_tp // CORES
    count, feat = tokens.shape
    slots, ff = cotangent.shape[2:]
    capacity = slots // n_ctx
    cols, half = ff // PARTS, feat // HI

    dma = pltpu.SemaphoreType.DMA
    def wide(rows, height):
        return jnp.pad(rows, ((0, height - rows.shape[0]), (0, ff - rows.shape[1])))

    small = jnp.concatenate([cotangent[0, 0], wide(tokens, count), wide(expert_ids.T.astype(BF16), 16)])
    out = pl.pallas_call(
        functools.partial(kernel, (n_z, n_ctx, n_lo, capacity)),
        out_shape=jax.ShapeDtypeStruct((slots + half + count, ff), BF16),
        in_specs=[pl.BlockSpec(memory_space=pl.ANY)] * 2,
        out_specs=pl.BlockSpec(memory_space=pl.ANY),
        scratch_shapes=[
            pltpu.VMEM((slots, ff), BF16),
            pltpu.VMEM((half, ff), BF16),
            pltpu.VMEM((count, feat), BF16),
            pltpu.VMEM((count, feat), BF16),
            pltpu.VMEM((16, LANES), BF16),
            pltpu.VMEM((slots, ff), BF16),
            pltpu.VMEM((feat // LANES + 1, n_ctx * ROWS, count), BF16),
            pltpu.VMEM((feat, n_z * slots), BF16),
            pltpu.VMEM(weights.shape[1:], BF16),
            pltpu.VMEM((n_ctx, ROWS, feat + LANES), BF16),
            pltpu.VMEM((n_ctx, ROWS, feat + LANES), BF16),
            pltpu.VMEM((n_tp, slots, feat), BF16),
            pltpu.VMEM((n_z, slots, feat), BF16),
            pltpu.VMEM((PARTS, slots, cols), F32),
            pltpu.VMEM((PARTS, n_z, slots, cols), BF16),
            pltpu.VMEM((n_lo, slots, feat), BF16),
            pltpu.VMEM((n_lo, slots, feat), BF16),
            pltpu.VMEM((n_lo, slots, feat), BF16),
            pltpu.VMEM((n_lo, slots, feat), BF16),
            pltpu.VMEM((n_ctx, ROWS, feat + LANES), BF16),
            pltpu.VMEM((n_ctx, ROWS, feat + LANES), BF16),
            pltpu.VMEM((PARTS, half, cols), BF16),
            pltpu.VMEM((PARTS, half, cols), F32),
            pltpu.VMEM((PARTS, half, cols), BF16),
            dma((4,)), dma((2 + PARTS,)),
            dma((n_ctx - 1,)), dma((n_ctx - 1,)),
            dma((n_lo,)), dma((n_lo,)),
            dma((n_lo,)), dma((n_lo,)),
            dma((n_lo,)), dma((2, n_z - 1)), dma((n_z,)),
            dma((2, PARTS, n_z // 2)), dma((2, PARTS, n_z // 2)),
            dma((n_lo,)), dma((n_lo,)),
            dma((n_lo,)), dma((n_lo,)),
            dma((n_ctx - 1,)), dma((n_ctx - 1,)),
            dma((PARTS,)), dma((PARTS,)),
        ],
        compiler_params=pltpu.CompilerParams(
            collective_id=0, has_side_effects=True, vmem_limit_bytes=48 * 1024 * 1024
        ),
    )(small, weights[0])
    return out[None, None, :slots], out[None, slots:slots + half], out[slots + half:, :feat]


def solution(mesh):
    placed = (
        P(("dp", "ctx"), "tp"),
        P(("dp", "ctx"), None),
        P("ctx", None, "tp"),
        P("dp", "ctx", None, "tp"),
    )
    return jax.shard_map(
        per_device,
        mesh=mesh,
        in_specs=placed,
        out_specs=(P("dp", "ctx", None, "tp"), P("ctx", "dp", "tp"), P(("dp", "ctx"), "tp")),
        check_vma=False,
    )
```
